32 devices in a mesh: lat: 4 (over y, x), lon: 8 (over z, core).
Axes of the slice: x: 2, y: 2, z: 4, core: 2. Of those that a mesh axis runs over, the one named last changes fastest.
Arguments:
- atmosphere: float32 [128, 1536, 256], P('lat', 'lon'), may hold values from -6 to 6
- cutoff_table: int32 [128], P('lat'), may hold values from 1 to 768, as said below
Outputs:
- advanced: float32 [128, 1536, 256], P('lat', 'lon')
The draws below stay inside these ranges and needn't reach their ends.
Inputs may be any that keep to these rules, and one draw needn't show every extreme that they name: `cutoff_table`: rows that lie 16 or more rows from both poles hold 768 and are left unfiltered; a row of a cap holds at most 34, and the cap row farthest from its pole holds exactly 34.
All inputs are finite; a program needn't handle non-finite values.
Results may differ from the reference program's by a relative error of at most 0.00005.
Values sent between devices are 32-bit elements; how exact they have to be, the bound alone decides.
A program may use at most 128 MiB of HBM per device.

```python
import jax
import jax.numpy as jnp
from jax import lax

NLON = 1536
LEV = 32
NLAT = 128
CHANNELS = 256
POLAR = 16
CMAX = 34


def draw_cutoff_table(key, part):
    rows = jnp.arange(NLAT)
    distance = jnp.minimum(rows, NLAT - 1 - rows)
    jitter = jax.random.randint(key, (NLAT,), 0, 4)
    values = 2 * distance + 1 + jitter
    values = jnp.where(distance == POLAR - 1, CMAX, values)
    values = jnp.where(distance < POLAR, values, NLON // 2)
    return values.astype(jnp.int32)


def steps_of(key, extent, split, smallest, top_value):
    def one(position, blocks):
        steps = jax.random.uniform(jax.random.fold_in(jax.random.fold_in(key, 6), position), (blocks,), jnp.float32, smallest / len(split), top_value / len(split))
        return jnp.repeat(jnp.exp(steps), extent[position] // blocks).reshape((-1,) + (1,) * (len(extent) - position - 1))

    gain = one(*split[0])
    for cut in split[1:]:
        gain = gain * one(*cut)
    return gain


def bell_draw(stream_key, dims, scale, bound, shards=(), held_as=jnp.bfloat16):
    values = jax.random.normal(stream_key, dims, jnp.float32) * scale
    if len(shards) > 0:
        values = steps_of(stream_key, dims, shards, -0.22, 0.18) * values
    return jnp.clip(values, min=-bound, max=bound).astype(held_as)


def setup_inputs(seed: int = 0) -> dict:
    key_list = jax.random.split(jax.random.key(seed), 3)
    atmosphere = bell_draw(key_list[0], (NLAT, NLON, CHANNELS), 1.0, 6.0, ((0, 4), (1, 8)), jnp.float32)
    cutoff_table = draw_cutoff_table(jax.random.fold_in(key_list[2], 71), 0)
    return {"atmosphere": atmosphere, "cutoff_table": cutoff_table}


courant_zonal = 0.5
courant_meridional = 0.5
diffusion_rate = 0.25
coriolis_rate = 1.0
time_step = 0.1


def tendency_parts(grid, rows, total_lat):
    centre = grid[1:-1, 1:-1]
    east_cell = grid[1:-1, 2:]
    west_cell = grid[1:-1, :-2]
    north_cell = grid[:-2, 1:-1]
    south_cell = grid[2:, 1:-1]
    spacing = jnp.pi / total_lat
    row_float = rows.astype(jnp.float32)
    cos_mid = jnp.sin((row_float + 0.5) * spacing)[:, None, None, None]
    sin_mid = jnp.cos((row_float + 0.5) * spacing)[:, None, None, None]
    cos_north = jnp.sin(row_float * spacing)[:, None, None, None]
    cos_south = jnp.sin((row_float + 1.0) * spacing)[:, None, None, None]
    flux_east = 0.5 * (centre[:, :, 0:1] + east_cell[:, :, 0:1]) * (0.5 * (centre + east_cell))
    flux_west = 0.5 * (west_cell[:, :, 0:1] + centre[:, :, 0:1]) * (0.5 * (west_cell + centre))
    flux_north = 0.5 * (north_cell[:, :, 1:2] + centre[:, :, 1:2]) * cos_north * (0.5 * (north_cell + centre))
    flux_south = 0.5 * (centre[:, :, 1:2] + south_cell[:, :, 1:2]) * cos_south * (0.5 * (centre + south_cell))
    spread = (courant_zonal * (flux_east - flux_west) + courant_meridional * (flux_north - flux_south)) / cos_mid
    smooth = diffusion_rate * (north_cell + south_cell - 2.0 * centre)
    turning = coriolis_rate * sin_mid * jnp.concatenate(
        [centre[:, :, 1:2], -centre[:, :, 0:1], jnp.zeros_like(centre[:, :, 2:])], axis=2)
    return spread, smooth + turning


def polar_filter(flat, cutoff_table):
    spectrum = jnp.fft.rfft(flat, axis=1)
    keep = jnp.arange(NLON // 2 + 1)[None, :, None] < cutoff_table[:, None, None]
    smoothed = jnp.fft.irfft(jnp.where(keep, spectrum, 0.0), n=NLON, axis=1).astype(flat.dtype)
    return jnp.where((cutoff_table >= NLON // 2)[:, None, None], flat, smoothed)


def level_step(layer, cutoff_table):
    cell = layer[..., None]
    flip = jnp.array([-1.0, -1.0, 1.0, 1.0, 1.0, 1.0, 1.0, 1.0], dtype=jnp.float32)[:, None]
    north_ghost = jnp.roll(cell[0], NLON // 2, axis=0) * flip
    south_ghost = jnp.roll(cell[-1], NLON // 2, axis=0) * flip
    extended = jnp.concatenate([north_ghost[None], cell, south_ghost[None]], axis=0)
    grid = jnp.concatenate([extended[:, -1:], extended, extended[:, :1]], axis=1)
    spread, rest = tendency_parts(grid, jnp.arange(NLAT), NLAT)
    filtered = polar_filter(spread[..., 0], cutoff_table)
    return layer + time_step * (rest[..., 0] - filtered)


def reference(atmosphere, cutoff_table):
    stacked = jnp.transpose(atmosphere.reshape(NLAT, NLON, 8, LEV), (3, 0, 1, 2))
    result = lax.map(lambda layer: level_step(layer, cutoff_table), stacked)
    return jnp.transpose(result, (1, 2, 3, 0)).reshape(NLAT, NLON, 8 * LEV)
```

```python
import functools
import math

import jax
import jax.numpy as jnp
import ml_dtypes
import numpy as np
from jax import lax
from jax.experimental import pallas as pl
from jax.experimental.pallas import tpu as pltpu
from jax.sharding import PartitionSpec as P

CMAX = 34
POLAR = 16
CHUNKS = POLAR // 2
COEF = 72
PAD = 8
MESH = pl.DeviceIdType.MESH

courant_zonal = 0.5
courant_meridional = 0.5
diffusion_rate = 0.25
coriolis_rate = 1.0
time_step = 0.1


def row_table(total_lat):
    rows = np.arange(total_lat, dtype=np.float64)
    spacing = np.pi / total_lat
    cos_mid = np.sin((rows + 0.5) * spacing)
    zonal = 0.25 * courant_zonal / cos_mid
    north = 0.25 * courant_meridional * np.sin(rows * spacing) / cos_mid
    south = 0.25 * courant_meridional * np.sin((rows + 1.0) * spacing) / cos_mid
    turning = time_step * coriolis_rate * np.cos((rows + 0.5) * spacing)
    return np.concatenate([zonal, north, south, turning]).astype(np.float32)


def split16(values):
    high = values.astype(ml_dtypes.bfloat16)
    low = (values - high.astype(np.float64)).astype(ml_dtypes.bfloat16)
    return high, low


def fourier_tables(lon_count, cols):
    total = lon_count * cols
    modes = np.arange(CMAX)
    phase = modes[:, None] * np.arange(total)[None, :] % total
    angles = phase * (2.0 * math.pi / total)
    rows = np.zeros((COEF, total))
    rows[:CMAX] = np.cos(angles)
    rows[CMAX : 2 * CMAX] = np.sin(angles)
    factor = np.zeros((COEF,))
    factor[:CMAX] = np.where(modes == 0, 1.0, 2.0) / total
    factor[CMAX : 2 * CMAX] = factor[:CMAX]
    per_device = rows.reshape(COEF, lon_count, cols).transpose(1, 0, 2)
    high, low = split16(per_device)
    forward = np.concatenate([high, low], axis=1)
    high, low = split16(time_step * (per_device * factor[None, :, None]).transpose(0, 2, 1))
    padded_cols = -(-cols // 16) * 16
    inverse = np.zeros((lon_count, padded_cols, 256), ml_dtypes.bfloat16)
    inverse[:, :cols, :COEF] = high
    inverse[:, :cols, COEF : 2 * COEF] = low
    inverse[:, :cols, 2 * COEF : 3 * COEF] = high
    return forward, inverse


def kernel(
    lat_count, lon_count, levels,
    atm, cuts, table, fwd_hbm, inv_hbm, out,
    grid, stage, spread, fwd, inv, ew_send, ew_recv,
    part, part_in, acc, from_outer, from_inner, total, other_total,
    load_sem, out_sem, tab_sem, halo_send, halo_recv, side_send, side_recv,
    part_send, part_recv, inner_send, outer_send, outer_recv, inner_recv, tot_send, tot_recv,
):
    rows, cols, chans = atm.shape
    lat, lon = lax.axis_index("lat"), lax.axis_index("lon")
    total_lat = lat_count * rows
    block = math.gcd(cols, 48)
    chips = lon_count // 2
    half = chips // 2
    chip, core = lon // 2, lon % 2
    is_right = chip // half
    depth = (1 - is_right) * chip + is_right * (chips - 1 - chip)
    step = 2 - 4 * is_right
    inner = lon + step
    outer = lon - step
    sibling = lon + 1 - 2 * core
    innermost = depth == half - 1
    last = lat // (lat_count - 1)
    polar = jnp.logical_or(lat == 0, lat == lat_count - 1)
    behind = (lon + lon_count // 2) % lon_count

    def wrap(offset):
        return (lon + lon_count + offset) % lon_count

    barrier = pltpu.get_barrier_semaphore()
    for other in (wrap(1), wrap(-1), wrap(2), wrap(-2), behind):
        pl.semaphore_signal(barrier, inc=1, device_id=(lat, other), device_id_type=MESH)

    @pl.when(lat > 0)
    def _():
        pl.semaphore_signal(barrier, inc=1, device_id=(lat - 1, lon), device_id_type=MESH)

    @pl.when(lat < lat_count - 1)
    def _():
        pl.semaphore_signal(barrier, inc=1, device_id=(lat + 1, lon), device_id_type=MESH)

    load = pltpu.make_async_copy(atm, grid.at[pl.ds(1, rows), pl.ds(PAD, cols)], load_sem)
    load.start()

    @pl.when(polar)
    def _():
        pltpu.make_async_copy(fwd_hbm.at[lon], fwd, tab_sem.at[0]).start()
        pltpu.make_async_copy(inv_hbm.at[lon], inv, tab_sem.at[1]).start()

    ends = (lat == 0).astype(jnp.int32) + (lat == lat_count - 1).astype(jnp.int32)
    pl.semaphore_wait(barrier, 7 - ends)

    def remote(src, dst, send, recv, to_lat, to_lon):
        return pltpu.make_async_remote_copy(
            src_ref=src, dst_ref=dst, send_sem=send, recv_sem=recv,
            device_id=(to_lat, to_lon), device_id_type=MESH,
        )

    def row_copy(source_row, ghost_row, send_slot, recv_slot, to_lat, to_lon):
        return remote(
            atm.at[source_row], grid.at[ghost_row, pl.ds(PAD, cols)],
            halo_send.at[send_slot], halo_recv.at[recv_slot], to_lat, to_lon,
        )

    @pl.when(lat == 0)
    def _():
        row_copy(0, 0, 0, 0, lat, behind).start()

    @pl.when(lat > 0)
    def _():
        row_copy(0, rows + 1, 0, 1, lat - 1, lon).start()

    @pl.when(lat < lat_count - 1)
    def _():
        row_copy(rows - 1, 0, 1, 0, lat + 1, lon).start()

    @pl.when(lat == lat_count - 1)
    def _():
        row_copy(rows - 1, rows + 1, 1, 1, lat, behind).start()

    load.wait()
    ew_send[0] = grid[1 : rows + 1, PAD : PAD + 1, :]
    ew_send[1] = grid[1 : rows + 1, PAD + cols - 1 : PAD + cols, :]
    to_west = remote(ew_send.at[0], ew_recv.at[1], side_send.at[0], side_recv.at[1], lat, wrap(-1))
    to_east = remote(ew_send.at[1], ew_recv.at[0], side_send.at[1], side_recv.at[0], lat, wrap(1))
    to_west.start()
    to_east.start()
    to_west.wait_recv()
    to_east.wait_recv()
    grid[1 : rows + 1, PAD - 1 : PAD, :] = ew_recv[0]
    grid[1 : rows + 1, PAD + cols : PAD + cols + 1, :] = ew_recv[1]

    lane = lax.broadcasted_iota(jnp.int32, (block, 128), 1)
    is_u = lane < levels
    is_v = jnp.logical_and(lane >= levels, lane < 2 * levels)

    def repeated(value, mask):
        value = jnp.where(mask, value, 0.0)
        value = value + pltpu.roll(value, levels, 1)
        return value + pltpu.roll(value, 2 * levels, 1)

    def wait_ghost(side):
        row_copy(0, side * (rows + 1), side, side, lat, lon_count - 1 - lon).wait_recv()

    def flip_ghost(row):
        winds = grid[row, PAD : PAD + cols, 0:128]
        lanes = lax.broadcasted_iota(jnp.int32, (cols, 128), 1)
        grid[row, PAD : PAD + cols, 0:128] = jnp.where(lanes < 2 * levels, -winds, winds)

    def row_step(i, filtered):
        row = lat * rows + i
        zonal = table[row]
        north = table[total_lat + row]
        south = table[2 * total_lat + row]
        turn = table[3 * total_lat + row]
        for first in range(PAD, PAD + cols, block):
            winds = None
            for h in range(chans // 128):
                lanes = slice(h * 128, h * 128 + 128)
                q = grid[i + 1, first : first + block, lanes]
                q_n = grid[i, first : first + block, lanes]
                q_s = grid[i + 2, first : first + block, lanes]
                east = q + grid[i + 1, first + 1 : first + 1 + block, lanes]
                west = q + grid[i + 1, first - 1 : first - 1 + block, lanes]
                above = q + q_n
                below = q + q_s
                base = (1.0 - 4.0 * diffusion_rate * time_step) * q
                base = base + (diffusion_rate * time_step) * (above + below)
                if h == 0:
                    winds = (
                        repeated(zonal * east, is_u), repeated(zonal * west, is_u),
                        repeated(north * above, is_v), repeated(south * below, is_v),
                    )
                    v = pltpu.roll(q, 128 - levels, 1)
                    u = pltpu.roll(q, levels, 1)
                    base = base + turn * jnp.where(is_u, v, jnp.where(is_v, -u, 0.0))
                u_e, u_w, v_n, v_s = winds
                value = (u_e * east - u_w * west) + (v_n * above - v_s * below)
                columns = slice(first - PAD, first - PAD + block)
                if filtered:
                    stage[i, columns, lanes] = base
                    spread[columns, lanes] = value
                else:
                    stage[i, columns, lanes] = base - time_step * value

    def send_row(i):
        pltpu.make_async_copy(stage.at[i], out.at[i], out_sem).start()

    def plain_row(i):
        row_step(i, False)
        send_row(i)

    def coefficients(i):
        row_step(i, True)
        value = spread[...]
        high = value.astype(jnp.bfloat16)
        low = (value - high.astype(jnp.float32)).astype(jnp.bfloat16)
        weights = fwd[...]
        both = jnp.dot(weights, high, preferred_element_type=jnp.float32)
        both = both + jnp.dot(weights, low, preferred_element_type=jnp.float32)
        return both[:COEF] + both[COEF:]

    def finish_row(i, coef):
        index = lax.broadcasted_iota(jnp.int32, (COEF, chans), 0)
        mode = jnp.where(index < CMAX, index, index - CMAX)
        coef = jnp.where(mode < cuts[i], coef, 0.0)
        high = coef.astype(jnp.bfloat16).astype(jnp.float32)
        low = coef - high
        zeros = jnp.zeros((256 - 3 * COEF, chans), jnp.float32)
        right = jnp.concatenate([high, high, low, zeros], axis=0).astype(jnp.bfloat16)
        smoothed = jnp.dot(inv[...], right, preferred_element_type=jnp.float32)
        stage[i] = stage[i] - smoothed[:cols]
        send_row(i)

    @pl.when(jnp.logical_not(polar))
    def _():
        def body(i, carry):
            plain_row(i)
            return carry

        lax.fori_loop(1, rows - 1, body, 0)
        wait_ghost(0)
        wait_ghost(1)
        plain_row(0)
        plain_row(rows - 1)

    @pl.when(polar)
    def _():
        def polar_row(n):
            return (1 - last) * (POLAR - 1 - n) + last * (rows - POLAR + n)

        plain = rows - POLAR

        def other_row(n):
            return (1 - last) * (POLAR + n) + last * (plain - 1 - n)

        def part_copy(k):
            return remote(part.at[k], part_in.at[k], part_send.at[k], part_recv.at[k], lat, sibling)

        def outward_in(k):
            return remote(acc.at[k], from_outer.at[k], inner_send.at[k], outer_recv.at[k], lat, inner)

        def across(k):
            return remote(acc.at[k], from_inner.at[k], inner_send.at[k], inner_recv.at[k], lat, inner)

        def outward(k):
            return remote(total.at[k], from_inner.at[k], outer_send.at[k], inner_recv.at[k], lat, outer)

        def total_copy(k):
            return remote(total.at[k], other_total.at[k], tot_send.at[k], tot_recv.at[k], lat, sibling)

        pltpu.make_async_copy(fwd_hbm.at[lon], fwd, tab_sem.at[0]).wait()
        pltpu.make_async_copy(inv_hbm.at[lon], inv, tab_sem.at[1]).wait()

        def send_inner(k):
            @pl.when(innermost)
            def _():
                across(k).start()

            @pl.when(jnp.logical_not(innermost))
            def _():
                outward_in(k).start()

        def join_pair(k):
            part_copy(k).wait_recv()
            acc[k] = acc[k] + part_in[k]

            @pl.when(depth == 0)
            def _():
                send_inner(k)

        def forward(k, carry):
            @pl.when(k == CHUNKS - 1)
            def _():
                @pl.when(lat == 0)
                def _():
                    wait_ghost(0)
                    flip_ghost(0)

                @pl.when(lat == lat_count - 1)
                def _():
                    wait_ghost(1)
                    flip_ghost(rows + 1)

            part[k] = coefficients(polar_row(2 * k + 1 - core))
            part_copy(k).start()
            acc[k] = coefficients(polar_row(2 * k + core))

            @pl.when(k > 0)
            def _():
                join_pair(k - 1)

            return carry

        lax.fori_loop(0, CHUNKS, forward, 0)
        join_pair(CHUNKS - 1)

        def middle(k, carry):
            @pl.when(depth > 0)
            def _():
                outward_in(k).wait_recv()
                acc[k] = acc[k] + from_outer[k]
                send_inner(k)

            @pl.when(k == CHUNKS - 1)
            def _():
                @pl.when(lat == 0)
                def _():
                    wait_ghost(1)

                @pl.when(lat == lat_count - 1)
                def _():
                    wait_ghost(0)

            def one(n, inside):
                plain_row(other_row(n))
                return inside

            return lax.fori_loop(k * plain // CHUNKS, (k + 1) * plain // CHUNKS, one, carry)

        lax.fori_loop(0, CHUNKS, middle, 0)

        def finish(k):
            total_copy(k).wait_recv()
            finish_row(polar_row(2 * k + core), total[k])
            finish_row(polar_row(2 * k + 1 - core), other_total[k])

        def backward(k, carry):
            across(k).wait_recv()
            received = from_inner[k]
            total[k] = jnp.where(innermost, received + acc[k], received)
            total_copy(k).start()

            @pl.when(depth > 0)
            def _():
                outward(k).start()

            @pl.when(k > 0)
            def _():
                finish(k - 1)

            return carry

        lax.fori_loop(0, CHUNKS, backward, 0)
        finish(CHUNKS - 1)

        def drain(k, carry):
            part_copy(k).wait_send()
            across(k).wait_send()
            total_copy(k).wait_send()

            @pl.when(depth > 0)
            def _():
                outward(k).wait_send()

            return carry

        lax.fori_loop(0, CHUNKS, drain, 0)

    to_west.wait_send()
    to_east.wait_send()
    for slot in range(2):
        row_copy(0, 0, slot, slot, lat, behind).wait_send()
    pltpu.make_async_copy(stage, out, out_sem).wait()


def local(forward, inverse, table, lat_count, lon_count, atmosphere, cutoff_table):
    rows, cols, chans = atmosphere.shape
    coef = pltpu.VMEM((CHUNKS, COEF, chans), jnp.float32)
    any_space = pl.BlockSpec(memory_space=pl.ANY)
    scalars = pl.BlockSpec(memory_space=pltpu.SMEM)
    dma = pltpu.SemaphoreType.DMA
    return pl.pallas_call(
        functools.partial(kernel, lat_count, lon_count, chans // 8),
        out_shape=jax.ShapeDtypeStruct(atmosphere.shape, atmosphere.dtype),
        in_specs=[any_space, scalars, scalars, any_space, any_space],
        out_specs=any_space,
        scratch_shapes=[
            pltpu.VMEM((rows + 2, cols + 2 * PAD, chans), jnp.float32),
            pltpu.VMEM((rows, cols, chans), jnp.float32),
            pltpu.VMEM((cols, chans), jnp.float32),
            pltpu.VMEM(forward.shape[1:], jnp.bfloat16),
            pltpu.VMEM(inverse.shape[1:], jnp.bfloat16),
            pltpu.VMEM((2, rows, 1, chans), jnp.float32),
            pltpu.VMEM((2, rows, 1, chans), jnp.float32),
            coef, coef, coef, coef, coef, coef, coef,
            dma, dma, dma((2,)), dma((2,)), dma((2,)), dma((2,)), dma((2,)),
        ] + [dma((CHUNKS,))] * 8,
        compiler_params=pltpu.CompilerParams(
            collective_id=0, has_side_effects=True, vmem_limit_bytes=48 * 1024 * 1024
        ),
    )(atmosphere, cutoff_table, table, forward, inverse)


def solution(mesh):
    lat_count, lon_count = mesh.shape["lat"], mesh.shape["lon"]

    def whole(atmosphere, cutoff_table):
        total_lat, total_lon, _ = atmosphere.shape
        forward, inverse = fourier_tables(lon_count, total_lon // lon_count)
        body = functools.partial(
            local, jnp.asarray(forward), jnp.asarray(inverse),
            jnp.asarray(row_table(total_lat)), lat_count, lon_count,
        )
        return jax.shard_map(
            body, mesh=mesh, in_specs=(P("lat", "lon", None), P("lat")),
            out_specs=P("lat", "lon", None), check_vma=False,
        )(atmosphere, cutoff_table)

    return whole
```

```python
import functools
import math

import jax
import jax.numpy as jnp
import ml_dtypes
import numpy as np
from jax import lax
from jax.experimental import pallas as pl
from jax.experimental.pallas import tpu as pltpu
from jax.sharding import PartitionSpec as P

CMAX = 34
POLAR = 16
CHUNKS = POLAR // 2
LAG_OUTER, LAG_TOTAL, LAG_FINISH, LAG_PLAIN = 3, 7, 9, 8
COEF = 72
GROUP = 2
BLOCK = 192
PAD = 8
MESH = pl.DeviceIdType.MESH

courant_zonal = 0.5
courant_meridional = 0.5
diffusion_rate = 0.25
coriolis_rate = 1.0
time_step = 0.1


def row_table(total_lat):
    rows = np.arange(total_lat, dtype=np.float64)
    spacing = np.pi / total_lat
    cos_mid = np.sin((rows + 0.5) * spacing)
    zonal = 0.25 * courant_zonal / cos_mid
    north = 0.25 * courant_meridional * np.sin(rows * spacing)
    south = 0.25 * courant_meridional * np.sin((rows + 1.0) * spacing)
    turning = time_step * coriolis_rate * np.cos((rows + 0.5) * spacing)
    return np.concatenate([zonal, north, turning, south]).astype(np.float32)


def split16(values):
    high = values.astype(ml_dtypes.bfloat16)
    low = (values - high.astype(np.float64)).astype(ml_dtypes.bfloat16)
    return high, low


def fourier_tables(lon_count, cols):
    total = lon_count * cols
    modes = np.arange(CMAX)
    phase = modes[:, None] * np.arange(total)[None, :] % total
    angles = phase * (2.0 * math.pi / total)
    rows = np.zeros((COEF, total))
    rows[:CMAX] = np.cos(angles)
    rows[CMAX : 2 * CMAX] = np.sin(angles)
    factor = np.zeros((COEF,))
    factor[:CMAX] = np.where(modes == 0, 1.0, 2.0) / total
    factor[CMAX : 2 * CMAX] = factor[:CMAX]
    per_device = rows.reshape(COEF, lon_count, cols).transpose(1, 0, 2)
    high, low = split16(per_device)
    forward = np.concatenate([high, low], axis=1)
    high, low = split16(time_step * (per_device * factor[None, :, None]).transpose(0, 2, 1))
    padded_cols = -(-cols // 16) * 16
    inverse = np.zeros((lon_count, padded_cols, 256), ml_dtypes.bfloat16)
    inverse[:, :cols, :COEF] = high
    inverse[:, :cols, COEF : 2 * COEF] = low
    inverse[:, :cols, 2 * COEF : 3 * COEF] = high
    return forward, inverse


def kernel(
    lat_count, lon_count, levels,
    atm, cuts, table, fwd_hbm, inv_hbm, out,
    grid, stage, spread, fwd, inv, ew_send, ew_recv,
    part, part_in, acc, from_outer, from_inner, total, other_total,
    load_sem, out_sem, tab_sem, halo_send, halo_recv, side_send, side_recv,
    part_send, part_recv, inner_send, outer_send, outer_recv, inner_recv, tot_send, tot_recv,
):
    rows, cols, chans = atm.shape
    lat, lon = lax.axis_index("lat"), lax.axis_index("lon")
    total_lat = lat_count * rows
    block = math.gcd(cols, BLOCK)
    chips = lon_count // 2
    half = chips // 2
    chip, core = lon // 2, lon % 2
    is_right = chip // half
    depth = (1 - is_right) * chip + is_right * (chips - 1 - chip)
    step = 2 - 4 * is_right
    inner = lon + step
    outer = lon - step
    sibling = lon + 1 - 2 * core
    innermost = depth == half - 1
    last = lat // (lat_count - 1)
    polar = jnp.logical_or(lat == 0, lat == lat_count - 1)
    behind = (lon + lon_count // 2) % lon_count

    def wrap(offset):
        return (lon + lon_count + offset) % lon_count

    barrier = pltpu.get_barrier_semaphore()
    for other in (wrap(1), wrap(-1), wrap(2), wrap(-2), behind):
        pl.semaphore_signal(barrier, inc=1, device_id=(lat, other), device_id_type=MESH)

    @pl.when(lat > 0)
    def _():
        pl.semaphore_signal(barrier, inc=1, device_id=(lat - 1, lon), device_id_type=MESH)

    @pl.when(lat < lat_count - 1)
    def _():
        pl.semaphore_signal(barrier, inc=1, device_id=(lat + 1, lon), device_id_type=MESH)

    load = pltpu.make_async_copy(atm, grid.at[pl.ds(1, rows), pl.ds(PAD, cols)], load_sem)
    load.start()

    @pl.when(polar)
    def _():
        pltpu.make_async_copy(fwd_hbm.at[lon], fwd, tab_sem.at[0]).start()
        pltpu.make_async_copy(inv_hbm.at[lon], inv, tab_sem.at[1]).start()

    ends = (lat == 0).astype(jnp.int32) + (lat == lat_count - 1).astype(jnp.int32)
    pl.semaphore_wait(barrier, 7 - ends)

    def remote(src, dst, send, recv, to_lat, to_lon):
        return pltpu.make_async_remote_copy(
            src_ref=src, dst_ref=dst, send_sem=send, recv_sem=recv,
            device_id=(to_lat, to_lon), device_id_type=MESH,
        )

    def row_copy(source_row, ghost_row, send_slot, recv_slot, to_lat, to_lon):
        return remote(
            atm.at[source_row], grid.at[ghost_row, pl.ds(PAD, cols)],
            halo_send.at[send_slot], halo_recv.at[recv_slot], to_lat, to_lon,
        )

    @pl.when(lat == 0)
    def _():
        row_copy(0, 0, 0, 0, lat, behind).start()

    @pl.when(lat > 0)
    def _():
        row_copy(0, rows + 1, 0, 1, lat - 1, lon).start()

    @pl.when(lat < lat_count - 1)
    def _():
        row_copy(rows - 1, 0, 1, 0, lat + 1, lon).start()

    @pl.when(lat == lat_count - 1)
    def _():
        row_copy(rows - 1, rows + 1, 1, 1, lat, behind).start()

    load.wait()
    ew_send[0] = grid[1 : rows + 1, PAD : PAD + 1, :]
    ew_send[1] = grid[1 : rows + 1, PAD + cols - 1 : PAD + cols, :]
    to_west = remote(ew_send.at[0], ew_recv.at[1], side_send.at[0], side_recv.at[1], lat, wrap(-1))
    to_east = remote(ew_send.at[1], ew_recv.at[0], side_send.at[1], side_recv.at[0], lat, wrap(1))
    to_west.start()
    to_east.start()
    to_west.wait_recv()
    to_east.wait_recv()
    grid[1 : rows + 1, PAD - 1 : PAD, :] = ew_recv[0]
    grid[1 : rows + 1, PAD + cols : PAD + cols + 1, :] = ew_recv[1]

    def tiled(zonal_wind, meridional_wind):
        lane = lax.broadcasted_iota(jnp.int32, zonal_wind.shape, 1)
        both = jnp.where(lane < levels, zonal_wind, meridional_wind)
        both = jnp.where(lane < 2 * levels, both, pltpu.roll(both, 2 * levels, 1))
        swapped = pltpu.roll(both, levels, 1)
        even = (lane // levels) % 2 == 0
        return jnp.where(even, both, swapped), jnp.where(even, swapped, both)

    def wait_ghost(side):
        row_copy(0, side * (rows + 1), side, side, lat, lon_count - 1 - lon).wait_recv()

    def flip_ghost(row):
        winds = grid[row, PAD : PAD + cols, 0:128]
        lanes = lax.broadcasted_iota(jnp.int32, (cols, 128), 1)
        grid[row, PAD : PAD + cols, 0:128] = jnp.where(lanes < 2 * levels, -winds, winds)

    halves = [slice(h * 128, h * 128 + 128) for h in range(chans // 128)]

    def row_group(i, count, filtered):
        scalars = []
        for g in range(count):
            row = lat * rows + i + g
            scalars.append((table[row], table[total_lat + row], table[2 * total_lat + row]))
        south = [table[3 * total_lat + lat * rows + i + g] for g in range(count)]
        lane = lax.broadcasted_iota(jnp.int32, (1, 128), 1)
        kept = [None] * count
        for first in [0] + list(range(PAD, PAD + cols, block)):
            width = block if first else PAD
            own = slice(first, first + width)
            shifted = slice(first + 1, first + 1 + width)
            columns = slice(first - PAD, first - PAD + width)
            above = face_above = None
            if first:
                q_n = [grid[i, own, h] for h in halves]
                q = [grid[i + 1, own, h] for h in halves]
                above = [x + y for x, y in zip(q_n, q)]
                scale = scalars[0][1]
                _, v = tiled(above[0] * scale, above[0] * scale)
                face_above = [v * x for x in above]
            else:
                q = [grid[i + 1, own, h] for h in halves]
            for g in range(count):
                zonal, _, turn = scalars[g]
                east = [x + grid[i + 1 + g, shifted, h] for x, h in zip(q, halves)]
                q_s = [grid[i + 2 + g, own, h] for h in halves]
                below = [x + y for x, y in zip(q, q_s)]
                u, v = tiled(east[0] * zonal, below[0] * south[g])
                face_east = [u * x for x in east]
                if first:
                    face_below = [v * x for x in below]
                    for n, h in enumerate(halves):
                        joined = jnp.concatenate([kept[g][n], face_east[n]], axis=0)
                        face_west = pltpu.roll(joined, 1, 0)[PAD:]
                        value = (face_east[n] - face_west) + (face_above[n] - face_below[n]) * (
                            4.0 / courant_zonal * zonal
                        )
                        base = (1.0 - 4.0 * diffusion_rate * time_step) * q[n]
                        base = base + (diffusion_rate * time_step) * (above[n] + below[n])
                        if n == 0:
                            to_u = jnp.where(lane < levels, turn, 0.0)
                            to_v = jnp.where(
                                jnp.logical_and(lane >= levels, lane < 2 * levels), turn, 0.0
                            )
                            base = base + to_u * pltpu.roll(q[0], 128 - levels, 1)
                            base = base - to_v * pltpu.roll(q[0], levels, 1)
                        if filtered:
                            stage[i + g, columns, h] = base
                            spread[g, columns, h] = value
                        else:
                            stage[i + g, columns, h] = base - time_step * value
                    above, face_above = below, face_below
                kept[g] = [x[width - PAD :] for x in face_east]
                q = q_s

    def send_row(i):
        pltpu.make_async_copy(stage.at[i], out.at[i], out_sem).start()

    def plain_rows(i):
        row_group(i, GROUP, False)
        for g in range(GROUP):
            send_row(i + g)

    def coefficients(g):
        value = spread[g]
        high = value.astype(jnp.bfloat16)
        low = (value - high.astype(jnp.float32)).astype(jnp.bfloat16)
        weights = fwd[...]
        both = jnp.dot(weights, high, preferred_element_type=jnp.float32)
        both = both + jnp.dot(weights, low, preferred_element_type=jnp.float32)
        return both[:COEF] + both[COEF:]

    def finish_row(i, coef):
        index = lax.broadcasted_iota(jnp.int32, (COEF, chans), 0)
        mode = jnp.where(index < CMAX, index, index - CMAX)
        coef = jnp.where(mode < cuts[i], coef, 0.0)
        high = coef.astype(jnp.bfloat16).astype(jnp.float32)
        low = coef - high
        zeros = jnp.zeros((256 - 3 * COEF, chans), jnp.float32)
        right = jnp.concatenate([high, high, low, zeros], axis=0).astype(jnp.bfloat16)
        smoothed = jnp.dot(inv[...], right, preferred_element_type=jnp.float32)
        stage[i] = stage[i] - smoothed[:cols]
        send_row(i)

    @pl.when(jnp.logical_not(polar))
    def _():
        def body(i, carry):
            plain_rows(i * GROUP)
            return carry

        lax.fori_loop(1, rows // GROUP - 1, body, 0)
        wait_ghost(0)
        wait_ghost(1)

        def end(n, carry):
            plain_rows(n * (rows - GROUP))
            return carry

        lax.fori_loop(0, 2, end, 0)

    @pl.when(polar)
    def _():
        def polar_row(n):
            return (1 - last) * (POLAR - 1 - n) + last * (rows - POLAR + n)

        plain = rows - POLAR

        groups = plain // GROUP

        def other_rows(n):
            return (1 - last) * (POLAR + n * GROUP) + last * (plain - GROUP - n * GROUP)

        def part_copy(k):
            return remote(part.at[k], part_in.at[k], part_send.at[k], part_recv.at[k], lat, sibling)

        def outward_in(k):
            return remote(acc.at[k], from_outer.at[k], inner_send.at[k], outer_recv.at[k], lat, inner)

        def across(k):
            return remote(acc.at[k], from_inner.at[k], inner_send.at[k], inner_recv.at[k], lat, inner)

        def outward(k):
            return remote(total.at[k], from_inner.at[k], outer_send.at[k], inner_recv.at[k], lat, outer)

        def total_copy(k):
            return remote(total.at[k], other_total.at[k], tot_send.at[k], tot_recv.at[k], lat, sibling)

        pltpu.make_async_copy(fwd_hbm.at[lon], fwd, tab_sem.at[0]).wait()
        pltpu.make_async_copy(inv_hbm.at[lon], inv, tab_sem.at[1]).wait()

        def send_inner(k):
            @pl.when(innermost)
            def _():
                across(k).start()

            @pl.when(jnp.logical_not(innermost))
            def _():
                outward_in(k).start()

        def join_pair(k):
            part_copy(k).wait_recv()
            acc[k] = acc[k] + part_in[k]

            @pl.when(depth == 0)
            def _():
                send_inner(k)

        def forward(k):
            @pl.when(k == CHUNKS - 1)
            def _():
                @pl.when(lat == 0)
                def _():
                    wait_ghost(0)
                    flip_ghost(0)

                @pl.when(lat == lat_count - 1)
                def _():
                    wait_ghost(1)
                    flip_ghost(rows + 1)

            row_group((1 - last) * (POLAR - 2 - 2 * k) + last * (rows - POLAR + 2 * k), 2, True)
            mine = (1 - last) * (1 - core) + last * core
            part[k] = coefficients(1 - mine)
            part_copy(k).start()
            acc[k] = coefficients(mine)

        def join_outer(k):
            @pl.when(depth > 0)
            def _():
                outward_in(k).wait_recv()
                acc[k] = acc[k] + from_outer[k]
                send_inner(k)

        def backward(k):
            across(k).wait_recv()
            received = from_inner[k]
            total[k] = jnp.where(innermost, received + acc[k], received)
            total_copy(k).start()

            @pl.when(depth > 0)
            def _():
                outward(k).start()

        def finish(k):
            total_copy(k).wait_recv()
            finish_row(polar_row(2 * k + core), total[k])
            finish_row(polar_row(2 * k + 1 - core), other_total[k])

        def plain_part(k):
            @pl.when(k == CHUNKS - 1)
            def _():
                @pl.when(lat == 0)
                def _():
                    wait_ghost(1)

                @pl.when(lat == lat_count - 1)
                def _():
                    wait_ghost(0)

            def one(n, carry):
                plain_rows(other_rows(n))
                return carry

            lax.fori_loop(k * groups // CHUNKS, (k + 1) * groups // CHUNKS, one, 0)

        stages = (
            (0, forward), (1, join_pair), (LAG_OUTER, join_outer), (LAG_PLAIN, plain_part),
            (LAG_TOTAL, backward), (LAG_FINISH, finish),
        )

        def tick(t, carry):
            for lag, stage_of in stages:
                @pl.when(jnp.logical_and(t >= lag, t < lag + CHUNKS))
                def _():
                    stage_of(t - lag)

            return carry

        lax.fori_loop(0, CHUNKS + LAG_FINISH, tick, 0)

        def drain(k, carry):
            part_copy(k).wait_send()
            across(k).wait_send()
            total_copy(k).wait_send()

            @pl.when(depth > 0)
            def _():
                outward(k).wait_send()

            return carry

        lax.fori_loop(0, CHUNKS, drain, 0)

    to_west.wait_send()
    to_east.wait_send()
    for slot in range(2):
        row_copy(0, 0, slot, slot, lat, behind).wait_send()
    pltpu.make_async_copy(stage, out, out_sem).wait()


def local(forward, inverse, table, lat_count, lon_count, atmosphere, cutoff_table):
    rows, cols, chans = atmosphere.shape
    coef = pltpu.VMEM((CHUNKS, COEF, chans), jnp.float32)
    any_space = pl.BlockSpec(memory_space=pl.ANY)
    scalars = pl.BlockSpec(memory_space=pltpu.SMEM)
    dma = pltpu.SemaphoreType.DMA
    return pl.pallas_call(
        functools.partial(kernel, lat_count, lon_count, chans // 8),
        out_shape=jax.ShapeDtypeStruct(atmosphere.shape, atmosphere.dtype),
        in_specs=[any_space, scalars, scalars, any_space, any_space],
        out_specs=any_space,
        scratch_shapes=[
            pltpu.VMEM((rows + 2, cols + 2 * PAD, chans), jnp.float32),
            pltpu.VMEM((rows, cols, chans), jnp.float32),
            pltpu.VMEM((2, cols, chans), jnp.float32),
            pltpu.VMEM(forward.shape[1:], jnp.bfloat16),
            pltpu.VMEM(inverse.shape[1:], jnp.bfloat16),
            pltpu.VMEM((2, rows, 1, chans), jnp.float32),
            pltpu.VMEM((2, rows, 1, chans), jnp.float32),
            coef, coef, coef, coef, coef, coef, coef,
            dma, dma, dma((2,)), dma((2,)), dma((2,)), dma((2,)), dma((2,)),
        ] + [dma((CHUNKS,))] * 8,
        compiler_params=pltpu.CompilerParams(
            collective_id=0, has_side_effects=True, vmem_limit_bytes=60 * 1024 * 1024
        ),
    )(atmosphere, cutoff_table, table, forward, inverse)


def solution(mesh):
    lat_count, lon_count = mesh.shape["lat"], mesh.shape["lon"]

    def whole(atmosphere, cutoff_table):
        total_lat, total_lon, _ = atmosphere.shape
        forward, inverse = fourier_tables(lon_count, total_lon // lon_count)
        body = functools.partial(
            local, jnp.asarray(forward), jnp.asarray(inverse),
            jnp.asarray(row_table(total_lat)), lat_count, lon_count,
        )
        return jax.shard_map(
            body, mesh=mesh, in_specs=(P("lat", "lon", None), P("lat")),
            out_specs=P("lat", "lon", None), check_vma=False,
        )(atmosphere, cutoff_table)

    return whole
```

```python
import functools
import math

import jax
import jax.numpy as jnp
import ml_dtypes
import numpy as np
from jax import lax
from jax.experimental import pallas as pl
from jax.experimental.pallas import tpu as pltpu
from jax.sharding import PartitionSpec as P

CMAX = 34
POLAR = 16
CHUNKS = POLAR // 2
LAG_OUTER, LAG_TOTAL, LAG_FINISH, LAG_PLAIN = 4, 8, 11, 8
COEF = 72
GROUP = 2
BLOCK = 192
PIECES = 16
PAD = 8
MESH = pl.DeviceIdType.MESH

courant_zonal = 0.5
courant_meridional = 0.5
diffusion_rate = 0.25
coriolis_rate = 1.0
time_step = 0.1


def row_table(total_lat):
    rows = np.arange(total_lat, dtype=np.float64)
    spacing = np.pi / total_lat
    cos_mid = np.sin((rows + 0.5) * spacing)
    zonal = 0.25 * courant_zonal / cos_mid
    north = 0.25 * courant_meridional * np.sin(rows * spacing)
    south = 0.25 * courant_meridional * np.sin((rows + 1.0) * spacing)
    turning = time_step * coriolis_rate * np.cos((rows + 0.5) * spacing)
    return np.concatenate([zonal, north, turning, south]).astype(np.float32)


def split16(values):
    high = values.astype(ml_dtypes.bfloat16)
    low = (values - high.astype(np.float64)).astype(ml_dtypes.bfloat16)
    return high, low


def fourier_tables(lon_count, cols):
    total = lon_count * cols
    modes = np.arange(CMAX)
    phase = modes[:, None] * np.arange(total)[None, :] % total
    angles = phase * (2.0 * math.pi / total)
    rows = np.zeros((COEF, total))
    rows[:CMAX] = np.cos(angles)
    rows[CMAX : 2 * CMAX] = np.sin(angles)
    factor = np.zeros((COEF,))
    factor[:CMAX] = np.where(modes == 0, 1.0, 2.0) / total
    factor[CMAX : 2 * CMAX] = factor[:CMAX]
    per_device = rows.reshape(COEF, lon_count, cols).transpose(1, 0, 2)
    high, low = split16(per_device)
    forward = np.concatenate([high, low], axis=1)
    high, low = split16(time_step * (per_device * factor[None, :, None]).transpose(0, 2, 1))
    padded_cols = -(-cols // 16) * 16
    inverse = np.zeros((lon_count, padded_cols, 256), ml_dtypes.bfloat16)
    inverse[:, :cols, :COEF] = high
    inverse[:, :cols, COEF : 2 * COEF] = low
    inverse[:, :cols, 2 * COEF : 3 * COEF] = high
    return forward, inverse


def kernel(
    lat_count, lon_count, levels,
    atm, cuts, table, fwd_hbm, inv_hbm, out,
    grid, stage, spread, fwd, inv, ew_send, ew_recv,
    part, part_in, acc, from_outer, from_inner, total, other_total,
    load_sem, out_sem, tab_sem, halo_send, halo_recv, side_send, side_recv,
    part_send, part_recv, inner_send, outer_send, outer_recv, inner_recv, tot_send, tot_recv,
):
    rows, cols, chans = atm.shape
    lat, lon = lax.axis_index("lat"), lax.axis_index("lon")
    total_lat = lat_count * rows
    block = math.gcd(cols, BLOCK)
    chips = lon_count // 2
    half = chips // 2
    chip, core = lon // 2, lon % 2
    is_right = chip // half
    depth = (1 - is_right) * chip + is_right * (chips - 1 - chip)
    step = 2 - 4 * is_right
    inner = lon + step
    outer = lon - step
    sibling = lon + 1 - 2 * core
    innermost = depth == half - 1
    last = lat // (lat_count - 1)
    polar = jnp.logical_or(lat == 0, lat == lat_count - 1)
    behind = (lon + lon_count // 2) % lon_count

    def wrap(offset):
        return (lon + lon_count + offset) % lon_count

    barrier = pltpu.get_barrier_semaphore()
    for other in (wrap(1), wrap(-1), wrap(2), wrap(-2), behind):
        pl.semaphore_signal(barrier, inc=1, device_id=(lat, other), device_id_type=MESH)

    @pl.when(lat > 0)
    def _():
        pl.semaphore_signal(barrier, inc=1, device_id=(lat - 1, lon), device_id_type=MESH)

    @pl.when(lat < lat_count - 1)
    def _():
        pl.semaphore_signal(barrier, inc=1, device_id=(lat + 1, lon), device_id_type=MESH)

    load = pltpu.make_async_copy(atm, grid.at[pl.ds(1, rows), pl.ds(PAD, cols)], load_sem)
    load.start()

    @pl.when(polar)
    def _():
        pltpu.make_async_copy(fwd_hbm.at[lon], fwd, tab_sem.at[0]).start()
        pltpu.make_async_copy(inv_hbm.at[lon], inv, tab_sem.at[1]).start()

    ends = (lat == 0).astype(jnp.int32) + (lat == lat_count - 1).astype(jnp.int32)
    pl.semaphore_wait(barrier, 7 - ends)

    def remote(src, dst, send, recv, to_lat, to_lon):
        return pltpu.make_async_remote_copy(
            src_ref=src, dst_ref=dst, send_sem=send, recv_sem=recv,
            device_id=(to_lat, to_lon), device_id_type=MESH,
        )

    def row_copy(source_row, ghost_row, send_slot, recv_slot, to_lat, to_lon):
        return remote(
            atm.at[source_row], grid.at[ghost_row, pl.ds(PAD, cols)],
            halo_send.at[send_slot], halo_recv.at[recv_slot], to_lat, to_lon,
        )

    @pl.when(lat == 0)
    def _():
        row_copy(0, 0, 0, 0, lat, behind).start()

    @pl.when(lat > 0)
    def _():
        row_copy(0, rows + 1, 0, 1, lat - 1, lon).start()

    @pl.when(lat < lat_count - 1)
    def _():
        row_copy(rows - 1, 0, 1, 0, lat + 1, lon).start()

    @pl.when(lat == lat_count - 1)
    def _():
        row_copy(rows - 1, rows + 1, 1, 1, lat, behind).start()

    load.wait()
    ew_send[0] = grid[1 : rows + 1, PAD : PAD + 1, :]
    ew_send[1] = grid[1 : rows + 1, PAD + cols - 1 : PAD + cols, :]
    to_west = remote(ew_send.at[0], ew_recv.at[1], side_send.at[0], side_recv.at[1], lat, wrap(-1))
    to_east = remote(ew_send.at[1], ew_recv.at[0], side_send.at[1], side_recv.at[0], lat, wrap(1))
    to_west.start()
    to_east.start()
    to_west.wait_recv()
    to_east.wait_recv()
    grid[1 : rows + 1, PAD - 1 : PAD, :] = ew_recv[0]
    grid[1 : rows + 1, PAD + cols : PAD + cols + 1, :] = ew_recv[1]

    def tiled(zonal_wind, meridional_wind):
        lane = lax.broadcasted_iota(jnp.int32, zonal_wind.shape, 1)
        both = jnp.where(lane < levels, zonal_wind, meridional_wind)
        both = jnp.where(lane < 2 * levels, both, pltpu.roll(both, 2 * levels, 1))
        swapped = pltpu.roll(both, levels, 1)
        even = (lane // levels) % 2 == 0
        return jnp.where(even, both, swapped), jnp.where(even, swapped, both)

    def wait_ghost(side):
        row_copy(0, side * (rows + 1), side, side, lat, lon_count - 1 - lon).wait_recv()

    def flip_ghost(row):
        winds = grid[row, PAD : PAD + cols, 0:128]
        lanes = lax.broadcasted_iota(jnp.int32, (cols, 128), 1)
        grid[row, PAD : PAD + cols, 0:128] = jnp.where(lanes < 2 * levels, -winds, winds)

    halves = [slice(h * 128, h * 128 + 128) for h in range(chans // 128)]

    def row_group(i, count, filtered):
        scalars = []
        for g in range(count):
            row = lat * rows + i + g
            scalars.append((table[row], table[total_lat + row], table[2 * total_lat + row]))
        south = [table[3 * total_lat + lat * rows + i + g] for g in range(count)]
        lane = lax.broadcasted_iota(jnp.int32, (1, 128), 1)
        kept = [None] * count
        for first in [0] + list(range(PAD, PAD + cols, block)):
            width = block if first else PAD
            own = slice(first, first + width)
            shifted = slice(first + 1, first + 1 + width)
            columns = slice(first - PAD, first - PAD + width)
            above = face_above = None
            if first:
                q_n = [grid[i, own, h] for h in halves]
                q = [grid[i + 1, own, h] for h in halves]
                above = [x + y for x, y in zip(q_n, q)]
                scale = scalars[0][1]
                _, v = tiled(above[0] * scale, above[0] * scale)
                face_above = [v * x for x in above]
            else:
                q = [grid[i + 1, own, h] for h in halves]
            for g in range(count):
                zonal, _, turn = scalars[g]
                east = [x + grid[i + 1 + g, shifted, h] for x, h in zip(q, halves)]
                q_s = [grid[i + 2 + g, own, h] for h in halves]
                below = [x + y for x, y in zip(q, q_s)]
                u, v = tiled(east[0] * zonal, below[0] * south[g])
                face_east = [u * x for x in east]
                if first:
                    face_below = [v * x for x in below]
                    for n, h in enumerate(halves):
                        joined = jnp.concatenate([kept[g][n], face_east[n]], axis=0)
                        face_west = pltpu.roll(joined, 1, 0)[PAD:]
                        value = (face_east[n] - face_west) + (face_above[n] - face_below[n]) * (
                            4.0 / courant_zonal * zonal
                        )
                        base = (1.0 - 4.0 * diffusion_rate * time_step) * q[n]
                        base = base + (diffusion_rate * time_step) * (above[n] + below[n])
                        if n == 0:
                            to_u = jnp.where(lane < levels, turn, 0.0)
                            to_v = jnp.where(
                                jnp.logical_and(lane >= levels, lane < 2 * levels), turn, 0.0
                            )
                            base = base + to_u * pltpu.roll(q[0], 128 - levels, 1)
                            base = base - to_v * pltpu.roll(q[0], levels, 1)
                        if filtered:
                            stage[i + g, columns, h] = base
                            spread[g, columns, h] = value
                        else:
                            stage[i + g, columns, h] = base - time_step * value
                    above, face_above = below, face_below
                kept[g] = [x[width - PAD :] for x in face_east]
                q = q_s

    def send_row(i):
        pltpu.make_async_copy(stage.at[i], out.at[i], out_sem).start()

    def plain_rows(i):
        row_group(i, GROUP, False)
        for g in range(GROUP):
            send_row(i + g)

    def coefficients(g):
        value = spread[g]
        high = value.astype(jnp.bfloat16)
        low = (value - high.astype(jnp.float32)).astype(jnp.bfloat16)
        weights = fwd[...]
        both = jnp.dot(weights, high, preferred_element_type=jnp.float32)
        both = both + jnp.dot(weights, low, preferred_element_type=jnp.float32)
        return both[:COEF] + both[COEF:]

    def finish_row(i, coef):
        index = lax.broadcasted_iota(jnp.int32, (COEF, chans), 0)
        mode = jnp.where(index < CMAX, index, index - CMAX)
        coef = jnp.where(mode < cuts[i], coef, 0.0)
        high = coef.astype(jnp.bfloat16).astype(jnp.float32)
        low = coef - high
        zeros = jnp.zeros((256 - 3 * COEF, chans), jnp.float32)
        right = jnp.concatenate([high, high, low, zeros], axis=0).astype(jnp.bfloat16)
        smoothed = jnp.dot(inv[...], right, preferred_element_type=jnp.float32)
        stage[i] = stage[i] - smoothed[:cols]
        send_row(i)

    @pl.when(jnp.logical_not(polar))
    def _():
        def body(i, carry):
            plain_rows(i * GROUP)
            return carry

        lax.fori_loop(1, rows // GROUP - 1, body, 0)
        wait_ghost(0)
        wait_ghost(1)

        def end(n, carry):
            plain_rows(n * (rows - GROUP))
            return carry

        lax.fori_loop(0, 2, end, 0)

    @pl.when(polar)
    def _():
        def polar_row(n):
            return (1 - last) * (POLAR - 1 - n) + last * (rows - POLAR + n)

        plain = rows - POLAR

        groups = plain // GROUP

        def other_rows(n):
            return (1 - last) * (POLAR + n * GROUP) + last * (plain - GROUP - n * GROUP)

        def part_copy(k):
            return remote(part.at[k], part_in.at[k], part_send.at[k], part_recv.at[k], lat, sibling)

        def outward_in(k):
            return remote(acc.at[k], from_outer.at[k], inner_send.at[k], outer_recv.at[k], lat, inner)

        def across(k):
            return remote(acc.at[k], from_inner.at[k], inner_send.at[k], inner_recv.at[k], lat, inner)

        def outward(k):
            return remote(total.at[k], from_inner.at[k], outer_send.at[k], inner_recv.at[k], lat, outer)

        def total_copy(k):
            return remote(total.at[k], other_total.at[k], tot_send.at[k], tot_recv.at[k], lat, sibling)

        pltpu.make_async_copy(fwd_hbm.at[lon], fwd, tab_sem.at[0]).wait()
        pltpu.make_async_copy(inv_hbm.at[lon], inv, tab_sem.at[1]).wait()

        def send_inner(k):
            @pl.when(innermost)
            def _():
                across(k).start()

            @pl.when(jnp.logical_not(innermost))
            def _():
                outward_in(k).start()

        def join_pair(k):
            part_copy(k).wait_recv()
            acc[k] = acc[k] + part_in[k]

            @pl.when(depth == 0)
            def _():
                send_inner(k)

        def forward(k):
            @pl.when(k == CHUNKS - 1)
            def _():
                @pl.when(lat == 0)
                def _():
                    wait_ghost(0)
                    flip_ghost(0)

                @pl.when(lat == lat_count - 1)
                def _():
                    wait_ghost(1)
                    flip_ghost(rows + 1)

            row_group((1 - last) * (POLAR - 2 - 2 * k) + last * (rows - POLAR + 2 * k), 2, True)
            mine = (1 - last) * (1 - core) + last * core
            part[k] = coefficients(1 - mine)
            part_copy(k).start()
            acc[k] = coefficients(mine)

        def join_outer(k):
            @pl.when(depth > 0)
            def _():
                outward_in(k).wait_recv()
                acc[k] = acc[k] + from_outer[k]
                send_inner(k)

        def backward(k):
            across(k).wait_recv()
            received = from_inner[k]
            total[k] = jnp.where(innermost, received + acc[k], received)
            total_copy(k).start()

            @pl.when(depth > 0)
            def _():
                outward(k).start()

        def finish(k):
            total_copy(k).wait_recv()
            finish_row(polar_row(2 * k + core), total[k])
            finish_row(polar_row(2 * k + 1 - core), other_total[k])

        def plain_part(k):
            @pl.when(k == CHUNKS - 1)
            def _():
                @pl.when(lat == 0)
                def _():
                    wait_ghost(1)

                @pl.when(lat == lat_count - 1)
                def _():
                    wait_ghost(0)

            def one(n, carry):
                plain_rows(other_rows(n))
                return carry

            lax.fori_loop(k * groups // CHUNKS, (k + 1) * groups // CHUNKS, one, 0)

        stages = (
            (0, forward), (1, join_pair), (LAG_OUTER, join_outer), (LAG_PLAIN, plain_part),
            (LAG_TOTAL, backward), (LAG_FINISH, finish),
        )

        def tick(t, carry):
            for lag, stage_of in stages:
                @pl.when(jnp.logical_and(t >= lag, t < lag + CHUNKS))
                def _():
                    stage_of(t - lag)

            return carry

        lax.fori_loop(0, CHUNKS + LAG_FINISH, tick, 0)

        def drain(k, carry):
            part_copy(k).wait_send()
            across(k).wait_send()
            total_copy(k).wait_send()

            @pl.when(depth > 0)
            def _():
                outward(k).wait_send()

            return carry

        lax.fori_loop(0, CHUNKS, drain, 0)

    to_west.wait_send()
    to_east.wait_send()
    for slot in range(2):
        row_copy(0, 0, slot, slot, lat, behind).wait_send()
    pltpu.make_async_copy(stage, out, out_sem).wait()


def write_out(source, out, held, in_sems, out_sems):
    pieces = in_sems.shape[0]
    size = source.shape[0] // pieces
    loads, stores = [], []
    for n in range(pieces):
        part = pl.ds(n * size, size)
        loads.append(pltpu.make_async_copy(source.at[part], held.at[part], in_sems.at[n]))
        stores.append(pltpu.make_async_copy(held.at[part], out.at[part], out_sems.at[n]))
    for load in loads:
        load.start()
    for load, store in zip(loads, stores):
        load.wait()
        store.start()
    for store in stores:
        store.wait()


def local(forward, inverse, table, lat_count, lon_count, atmosphere, cutoff_table):
    rows, cols, chans = atmosphere.shape
    coef = pltpu.VMEM((CHUNKS, COEF, chans), jnp.float32)
    any_space = pl.BlockSpec(memory_space=pl.ANY)
    scalars = pl.BlockSpec(memory_space=pltpu.SMEM)
    dma = pltpu.SemaphoreType.DMA
    advanced = pl.pallas_call(
        functools.partial(kernel, lat_count, lon_count, chans // 8),
        out_shape=jax.ShapeDtypeStruct(atmosphere.shape, atmosphere.dtype),
        in_specs=[any_space, scalars, scalars, any_space, any_space],
        out_specs=any_space,
        scratch_shapes=[
            pltpu.VMEM((rows + 2, cols + 2 * PAD, chans), jnp.float32),
            pltpu.VMEM((rows, cols, chans), jnp.float32),
            pltpu.VMEM((2, cols, chans), jnp.float32),
            pltpu.VMEM(forward.shape[1:], jnp.bfloat16),
            pltpu.VMEM(inverse.shape[1:], jnp.bfloat16),
            pltpu.VMEM((2, rows, 1, chans), jnp.float32),
            pltpu.VMEM((2, rows, 1, chans), jnp.float32),
            coef, coef, coef, coef, coef, coef, coef,
            dma, dma, dma((2,)), dma((2,)), dma((2,)), dma((2,)), dma((2,)),
        ] + [dma((CHUNKS,))] * 8,
        compiler_params=pltpu.CompilerParams(
            collective_id=0, has_side_effects=True, vmem_limit_bytes=60 * 1024 * 1024
        ),
    )(atmosphere, cutoff_table, table, forward, inverse)
    pieces = math.gcd(rows, PIECES)
    return pl.pallas_call(
        write_out,
        out_shape=jax.ShapeDtypeStruct(atmosphere.shape, atmosphere.dtype),
        in_specs=[any_space],
        out_specs=any_space,
        scratch_shapes=[
            pltpu.VMEM((rows, cols, chans), jnp.float32), dma((pieces,)), dma((pieces,)),
        ],
        compiler_params=pltpu.CompilerParams(vmem_limit_bytes=60 * 1024 * 1024),
    )(advanced)


def solution(mesh):
    lat_count, lon_count = mesh.shape["lat"], mesh.shape["lon"]

    def whole(atmosphere, cutoff_table):
        total_lat, total_lon, _ = atmosphere.shape
        forward, inverse = fourier_tables(lon_count, total_lon // lon_count)
        body = functools.partial(
            local, jnp.asarray(forward), jnp.asarray(inverse),
            jnp.asarray(row_table(total_lat)), lat_count, lon_count,
        )
        return jax.shard_map(
            body, mesh=mesh, in_specs=(P("lat", "lon", None), P("lat")),
            out_specs=P("lat", "lon", None), check_vma=False,
        )(atmosphere, cutoff_table)

    return whole
```

```python
import functools
import math

import jax
import jax.numpy as jnp
import ml_dtypes
import numpy as np
from jax import lax
from jax.experimental import pallas as pl
from jax.experimental.pallas import tpu as pltpu
from jax.sharding import PartitionSpec as P

CMAX = 34
POLAR = 16
CHUNKS = POLAR // 2
LAG_OUTER, LAG_TOTAL, LAG_FINISH, LAG_PLAIN = 5, 9, 12, 8
COEF = 72
GROUP = 2
BLOCK = 192
PIECES = 16
PAD = 8
MESH = pl.DeviceIdType.MESH

courant_zonal = 0.5
courant_meridional = 0.5
diffusion_rate = 0.25
coriolis_rate = 1.0
time_step = 0.1


def row_table(total_lat):
    rows = np.arange(total_lat, dtype=np.float64)
    spacing = np.pi / total_lat
    cos_mid = np.sin((rows + 0.5) * spacing)
    zonal = 0.25 * courant_zonal / cos_mid
    north = 0.25 * courant_meridional * np.sin(rows * spacing)
    south = 0.25 * courant_meridional * np.sin((rows + 1.0) * spacing)
    turning = time_step * coriolis_rate * np.cos((rows + 0.5) * spacing)
    return np.concatenate([zonal, north, turning, south]).astype(np.float32)


def split16(values):
    high = values.astype(ml_dtypes.bfloat16)
    low = (values - high.astype(np.float64)).astype(ml_dtypes.bfloat16)
    return high, low


def fourier_tables(lon_count, cols):
    total = lon_count * cols
    modes = np.arange(CMAX)
    phase = modes[:, None] * np.arange(total)[None, :] % total
    angles = phase * (2.0 * math.pi / total)
    rows = np.zeros((COEF, total))
    rows[:CMAX] = np.cos(angles)
    rows[CMAX : 2 * CMAX] = np.sin(angles)
    factor = np.zeros((COEF,))
    factor[:CMAX] = np.where(modes == 0, 1.0, 2.0) / total
    factor[CMAX : 2 * CMAX] = factor[:CMAX]
    per_device = rows.reshape(COEF, lon_count, cols).transpose(1, 0, 2)
    high, low = split16(per_device)
    forward = np.concatenate([high, low], axis=1)
    high, low = split16(time_step * (per_device * factor[None, :, None]).transpose(0, 2, 1))
    padded_cols = -(-cols // 16) * 16
    inverse = np.zeros((lon_count, padded_cols, 256), ml_dtypes.bfloat16)
    inverse[:, :cols, :COEF] = high
    inverse[:, :cols, COEF : 2 * COEF] = low
    inverse[:, :cols, 2 * COEF : 3 * COEF] = high
    return forward, inverse


def kernel(
    lat_count, lon_count, levels,
    atm, cuts, table, fwd_hbm, inv_hbm, out,
    grid, stage, spread, fwd, inv, ew_send, ew_recv,
    part, part_in, acc, from_outer, from_inner, total, other_total,
    load_sem, out_sem, tab_sem, halo_send, halo_recv, side_send, side_recv,
    part_send, part_recv, inner_send, outer_send, outer_recv, inner_recv, tot_send, tot_recv,
):
    rows, cols, chans = atm.shape
    lat, lon = lax.axis_index("lat"), lax.axis_index("lon")
    total_lat = lat_count * rows
    block = math.gcd(cols, BLOCK)
    chips = lon_count // 2
    half = chips // 2
    chip, core = lon // 2, lon % 2
    is_right = chip // half
    depth = (1 - is_right) * chip + is_right * (chips - 1 - chip)
    step = 2 - 4 * is_right
    inner = lon + step
    outer = lon - step
    sibling = lon + 1 - 2 * core
    innermost = depth == half - 1
    last = lat // (lat_count - 1)
    polar = jnp.logical_or(lat == 0, lat == lat_count - 1)
    behind = (lon + lon_count // 2) % lon_count

    def wrap(offset):
        return (lon + lon_count + offset) % lon_count

    barrier = pltpu.get_barrier_semaphore()
    for other in (wrap(1), wrap(-1), wrap(2), wrap(-2), behind):
        pl.semaphore_signal(barrier, inc=1, device_id=(lat, other), device_id_type=MESH)

    @pl.when(lat > 0)
    def _():
        pl.semaphore_signal(barrier, inc=1, device_id=(lat - 1, lon), device_id_type=MESH)

    @pl.when(lat < lat_count - 1)
    def _():
        pl.semaphore_signal(barrier, inc=1, device_id=(lat + 1, lon), device_id_type=MESH)

    load = pltpu.make_async_copy(atm, grid.at[pl.ds(1, rows), pl.ds(PAD, cols)], load_sem)
    load.start()

    @pl.when(polar)
    def _():
        pltpu.make_async_copy(fwd_hbm.at[lon], fwd, tab_sem.at[0]).start()
        pltpu.make_async_copy(inv_hbm.at[lon], inv, tab_sem.at[1]).start()

    ends = (lat == 0).astype(jnp.int32) + (lat == lat_count - 1).astype(jnp.int32)
    pl.semaphore_wait(barrier, 7 - ends)

    def remote(src, dst, send, recv, to_lat, to_lon):
        return pltpu.make_async_remote_copy(
            src_ref=src, dst_ref=dst, send_sem=send, recv_sem=recv,
            device_id=(to_lat, to_lon), device_id_type=MESH,
        )

    def row_copy(source_row, ghost_row, send_slot, recv_slot, to_lat, to_lon):
        return remote(
            atm.at[source_row], grid.at[ghost_row, pl.ds(PAD, cols)],
            halo_send.at[send_slot], halo_recv.at[recv_slot], to_lat, to_lon,
        )

    @pl.when(lat == 0)
    def _():
        row_copy(0, 0, 0, 0, lat, behind).start()

    @pl.when(lat > 0)
    def _():
        row_copy(0, rows + 1, 0, 1, lat - 1, lon).start()

    @pl.when(lat < lat_count - 1)
    def _():
        row_copy(rows - 1, 0, 1, 0, lat + 1, lon).start()

    @pl.when(lat == lat_count - 1)
    def _():
        row_copy(rows - 1, rows + 1, 1, 1, lat, behind).start()

    load.wait()
    ew_send[0] = grid[1 : rows + 1, PAD : PAD + 1, :]
    ew_send[1] = grid[1 : rows + 1, PAD + cols - 1 : PAD + cols, :]
    to_west = remote(ew_send.at[0], ew_recv.at[1], side_send.at[0], side_recv.at[1], lat, wrap(-1))
    to_east = remote(ew_send.at[1], ew_recv.at[0], side_send.at[1], side_recv.at[0], lat, wrap(1))
    to_west.start()
    to_east.start()
    to_west.wait_recv()
    to_east.wait_recv()
    grid[1 : rows + 1, PAD - 1 : PAD, :] = ew_recv[0]
    grid[1 : rows + 1, PAD + cols : PAD + cols + 1, :] = ew_recv[1]

    def tiled(zonal_wind, meridional_wind):
        lane = lax.broadcasted_iota(jnp.int32, zonal_wind.shape, 1)
        both = jnp.where(lane < levels, zonal_wind, meridional_wind)
        both = jnp.where(lane < 2 * levels, both, pltpu.roll(both, 2 * levels, 1))
        swapped = pltpu.roll(both, levels, 1)
        even = (lane // levels) % 2 == 0
        return jnp.where(even, both, swapped), jnp.where(even, swapped, both)

    def wait_ghost(side):
        row_copy(0, side * (rows + 1), side, side, lat, lon_count - 1 - lon).wait_recv()

    def flip_ghost(row):
        winds = grid[row, PAD : PAD + cols, 0:128]
        lanes = lax.broadcasted_iota(jnp.int32, (cols, 128), 1)
        grid[row, PAD : PAD + cols, 0:128] = jnp.where(lanes < 2 * levels, -winds, winds)

    halves = [slice(h * 128, h * 128 + 128) for h in range(chans // 128)]

    def row_group(i, count, filtered):
        scalars = []
        for g in range(count):
            row = lat * rows + i + g
            scalars.append((table[row], table[total_lat + row], table[2 * total_lat + row]))
        south = [table[3 * total_lat + lat * rows + i + g] for g in range(count)]
        lane = lax.broadcasted_iota(jnp.int32, (1, 128), 1)
        kept = [None] * count
        for first in [0] + list(range(PAD, PAD + cols, block)):
            width = block if first else PAD
            own = slice(first, first + width)
            shifted = slice(first + 1, first + 1 + width)
            columns = slice(first - PAD, first - PAD + width)
            above = face_above = None
            if first:
                q_n = [grid[i, own, h] for h in halves]
                q = [grid[i + 1, own, h] for h in halves]
                above = [x + y for x, y in zip(q_n, q)]
                scale = scalars[0][1]
                _, v = tiled(above[0] * scale, above[0] * scale)
                face_above = [v * x for x in above]
            else:
                q = [grid[i + 1, own, h] for h in halves]
            for g in range(count):
                zonal, _, turn = scalars[g]
                east = [x + grid[i + 1 + g, shifted, h] for x, h in zip(q, halves)]
                q_s = [grid[i + 2 + g, own, h] for h in halves]
                below = [x + y for x, y in zip(q, q_s)]
                u, v = tiled(east[0] * zonal, below[0] * south[g])
                face_east = [u * x for x in east]
                if first:
                    face_below = [v * x for x in below]
                    for n, h in enumerate(halves):
                        joined = jnp.concatenate([kept[g][n], face_east[n]], axis=0)
                        face_west = pltpu.roll(joined, 1, 0)[PAD:]
                        value = (face_east[n] - face_west) + (face_above[n] - face_below[n]) * (
                            4.0 / courant_zonal * zonal
                        )
                        base = (1.0 - 4.0 * diffusion_rate * time_step) * q[n]
                        base = base + (diffusion_rate * time_step) * (above[n] + below[n])
                        if n == 0:
                            to_u = jnp.where(lane < levels, turn, 0.0)
                            to_v = jnp.where(
                                jnp.logical_and(lane >= levels, lane < 2 * levels), turn, 0.0
                            )
                            base = base + to_u * pltpu.roll(q[0], 128 - levels, 1)
                            base = base - to_v * pltpu.roll(q[0], levels, 1)
                        if filtered:
                            stage[i + g, columns, h] = base
                            spread[g, columns, h] = value
                        else:
                            stage[i + g, columns, h] = base - time_step * value
                    above, face_above = below, face_below
                kept[g] = [x[width - PAD :] for x in face_east]
                q = q_s

    def send_row(i):
        pltpu.make_async_copy(stage.at[i], out.at[i], out_sem).start()

    def plain_rows(i):
        row_group(i, GROUP, False)
        for g in range(GROUP):
            send_row(i + g)

    def coefficients(g):
        value = spread[g]
        high = value.astype(jnp.bfloat16)
        low = (value - high.astype(jnp.float32)).astype(jnp.bfloat16)
        weights = fwd[...]
        both = jnp.dot(weights, high, preferred_element_type=jnp.float32)
        both = both + jnp.dot(weights, low, preferred_element_type=jnp.float32)
        return both[:COEF] + both[COEF:]

    def finish_row(i, coef):
        index = lax.broadcasted_iota(jnp.int32, (COEF, chans), 0)
        mode = jnp.where(index < CMAX, index, index - CMAX)
        coef = jnp.where(mode < cuts[i], coef, 0.0)
        high = coef.astype(jnp.bfloat16).astype(jnp.float32)
        low = coef - high
        zeros = jnp.zeros((256 - 3 * COEF, chans), jnp.float32)
        right = jnp.concatenate([high, high, low, zeros], axis=0).astype(jnp.bfloat16)
        smoothed = jnp.dot(inv[...], right, preferred_element_type=jnp.float32)
        stage[i] = stage[i] - smoothed[:cols]
        send_row(i)

    @pl.when(jnp.logical_not(polar))
    def _():
        def body(i, carry):
            plain_rows(i * GROUP)
            return carry

        lax.fori_loop(1, rows // GROUP - 1, body, 0)
        wait_ghost(0)
        wait_ghost(1)

        def end(n, carry):
            plain_rows(n * (rows - GROUP))
            return carry

        lax.fori_loop(0, 2, end, 0)

    @pl.when(polar)
    def _():
        def polar_row(n):
            return (1 - last) * (POLAR - 1 - n) + last * (rows - POLAR + n)

        plain = rows - POLAR

        groups = plain // GROUP

        def other_rows(n):
            return (1 - last) * (POLAR + n * GROUP) + last * (plain - GROUP - n * GROUP)

        def part_copy(k):
            return remote(part.at[k], part_in.at[k], part_send.at[k], part_recv.at[k], lat, sibling)

        def outward_in(k):
            return remote(acc.at[k], from_outer.at[k], inner_send.at[k], outer_recv.at[k], lat, inner)

        def across(k):
            return remote(acc.at[k], from_inner.at[k], inner_send.at[k], inner_recv.at[k], lat, inner)

        def outward(k):
            return remote(total.at[k], from_inner.at[k], outer_send.at[k], inner_recv.at[k], lat, outer)

        def total_copy(k):
            return remote(total.at[k], other_total.at[k], tot_send.at[k], tot_recv.at[k], lat, sibling)

        pltpu.make_async_copy(fwd_hbm.at[lon], fwd, tab_sem.at[0]).wait()
        pltpu.make_async_copy(inv_hbm.at[lon], inv, tab_sem.at[1]).wait()

        def send_inner(k):
            @pl.when(innermost)
            def _():
                across(k).start()

            @pl.when(jnp.logical_not(innermost))
            def _():
                outward_in(k).start()

        def join_pair(k):
            part_copy(k).wait_recv()
            acc[k] = acc[k] + part_in[k]

            @pl.when(depth == 0)
            def _():
                send_inner(k)

        def forward(k):
            @pl.when(k == CHUNKS - 1)
            def _():
                @pl.when(lat == 0)
                def _():
                    wait_ghost(0)
                    flip_ghost(0)

                @pl.when(lat == lat_count - 1)
                def _():
                    wait_ghost(1)
                    flip_ghost(rows + 1)

            row_group((1 - last) * (POLAR - 2 - 2 * k) + last * (rows - POLAR + 2 * k), 2, True)
            mine = (1 - last) * (1 - core) + last * core
            part[k] = coefficients(1 - mine)
            part_copy(k).start()
            acc[k] = coefficients(mine)

        def join_outer(k):
            @pl.when(depth > 0)
            def _():
                outward_in(k).wait_recv()
                acc[k] = acc[k] + from_outer[k]
                send_inner(k)

        def backward(k):
            across(k).wait_recv()
            received = from_inner[k]
            total[k] = jnp.where(innermost, received + acc[k], received)
            total_copy(k).start()

            @pl.when(depth > 0)
            def _():
                outward(k).start()

        def finish(k):
            total_copy(k).wait_recv()
            finish_row(polar_row(2 * k + core), total[k])
            finish_row(polar_row(2 * k + 1 - core), other_total[k])

        def plain_part(k):
            @pl.when(k == CHUNKS - 1)
            def _():
                @pl.when(lat == 0)
                def _():
                    wait_ghost(1)

                @pl.when(lat == lat_count - 1)
                def _():
                    wait_ghost(0)

            def one(n, carry):
                plain_rows(other_rows(n))
                return carry

            lax.fori_loop(k * groups // CHUNKS, (k + 1) * groups // CHUNKS, one, 0)

        stages = (
            (0, forward), (1, join_pair), (LAG_OUTER, join_outer), (LAG_PLAIN, plain_part),
            (LAG_TOTAL, backward), (LAG_FINISH, finish),
        )

        def tick(t, carry):
            for lag, stage_of in stages:
                @pl.when(jnp.logical_and(t >= lag, t < lag + CHUNKS))
                def _():
                    stage_of(t - lag)

            return carry

        lax.fori_loop(0, CHUNKS + LAG_FINISH, tick, 0)

        def drain(k, carry):
            part_copy(k).wait_send()
            across(k).wait_send()
            total_copy(k).wait_send()

            @pl.when(depth > 0)
            def _():
                outward(k).wait_send()

            return carry

        lax.fori_loop(0, CHUNKS, drain, 0)

    to_west.wait_send()
    to_east.wait_send()
    for slot in range(2):
        row_copy(0, 0, slot, slot, lat, behind).wait_send()
    pltpu.make_async_copy(stage, out, out_sem).wait()


def write_out(source, out, held, in_sems, out_sems):
    pieces = in_sems.shape[0]
    size = source.shape[0] // pieces
    loads, stores = [], []
    for n in range(pieces):
        part = pl.ds(n * size, size)
        loads.append(pltpu.make_async_copy(source.at[part], held.at[part], in_sems.at[n]))
        stores.append(pltpu.make_async_copy(held.at[part], out.at[part], out_sems.at[n]))
    for load in loads:
        load.start()
    for load, store in zip(loads, stores):
        load.wait()
        store.start()
    for store in stores:
        store.wait()


def local(forward, inverse, table, lat_count, lon_count, atmosphere, cutoff_table):
    rows, cols, chans = atmosphere.shape
    coef = pltpu.VMEM((CHUNKS, COEF, chans), jnp.float32)
    any_space = pl.BlockSpec(memory_space=pl.ANY)
    scalars = pl.BlockSpec(memory_space=pltpu.SMEM)
    dma = pltpu.SemaphoreType.DMA
    advanced = pl.pallas_call(
        functools.partial(kernel, lat_count, lon_count, chans // 8),
        out_shape=jax.ShapeDtypeStruct(atmosphere.shape, atmosphere.dtype),
        in_specs=[any_space, scalars, scalars, any_space, any_space],
        out_specs=any_space,
        scratch_shapes=[
            pltpu.VMEM((rows + 2, cols + 2 * PAD, chans), jnp.float32),
            pltpu.VMEM((rows, cols, chans), jnp.float32),
            pltpu.VMEM((2, cols, chans), jnp.float32),
            pltpu.VMEM(forward.shape[1:], jnp.bfloat16),
            pltpu.VMEM(inverse.shape[1:], jnp.bfloat16),
            pltpu.VMEM((2, rows, 1, chans), jnp.float32),
            pltpu.VMEM((2, rows, 1, chans), jnp.float32),
            coef, coef, coef, coef, coef, coef, coef,
            dma, dma, dma((2,)), dma((2,)), dma((2,)), dma((2,)), dma((2,)),
        ] + [dma((CHUNKS,))] * 8,
        compiler_params=pltpu.CompilerParams(
            collective_id=0, has_side_effects=True, vmem_limit_bytes=60 * 1024 * 1024
        ),
    )(atmosphere, cutoff_table, table, forward, inverse)
    pieces = math.gcd(rows, PIECES)
    return pl.pallas_call(
        write_out,
        out_shape=jax.ShapeDtypeStruct(atmosphere.shape, atmosphere.dtype),
        in_specs=[any_space],
        out_specs=any_space,
        scratch_shapes=[
            pltpu.VMEM((rows, cols, chans), jnp.float32), dma((pieces,)), dma((pieces,)),
        ],
        compiler_params=pltpu.CompilerParams(vmem_limit_bytes=60 * 1024 * 1024),
    )(advanced)


def solution(mesh):
    lat_count, lon_count = mesh.shape["lat"], mesh.shape["lon"]

    def whole(atmosphere, cutoff_table):
        total_lat, total_lon, _ = atmosphere.shape
        forward, inverse = fourier_tables(lon_count, total_lon // lon_count)
        body = functools.partial(
            local, jnp.asarray(forward), jnp.asarray(inverse),
            jnp.asarray(row_table(total_lat)), lat_count, lon_count,
        )
        return jax.shard_map(
            body, mesh=mesh, in_specs=(P("lat", "lon", None), P("lat")),
            out_specs=P("lat", "lon", None), check_vma=False,
        )(atmosphere, cutoff_table)

    return whole
```
